32 devices in a mesh: wide: 8 (over y, x, core), narrow: 4 (over z).
Axes of the slice: x: 2, y: 2, z: 4, core: 2. Of those that a mesh axis runs over, the one named last changes fastest.
Arguments:
- raw_samples: bfloat16 [256, 8, 16384], P(('wide', 'narrow')), as said below
- filter_taps: float32 [64], replicated, may hold values from -0.75 to 0.75
- tile_pairs: int32 [16, 2], replicated, may hold values from 0 to 31, as said below
- tile_owners: int32 [16], replicated, may hold values from 0 to 3, as said below
Outputs:
- correlation_stacks: float32 [32, 64, 512], P('narrow', 'wide')
The draws below stay inside these ranges and needn't reach their ends.
Inputs may be any that keep to these rules, and one draw needn't show every extreme that they name: `raw_samples`: noise samples, scaled per channel and per window. `tile_pairs`: each row is (source block, receiver block), and the two blocks differ. `tile_owners`: each owner has at most 8 tiles, and some owner has exactly 8.
All inputs are finite; a program needn't handle non-finite values.
Results may differ from the reference program's by a relative error of at most 0.0074.
Values may be sent and summed in bfloat16 or wider, within the bound.
A program may use at most 128 MiB of HBM per device.

```python
import math
import jax
import jax.numpy as jnp
from jax import lax

NFFT = 4096
DECIM = 4
TAPS = 64
NBINS = 1024
SMOOTH = 63
LAGS = 512
BLK = 8
SLOTS = 8
RAW = 16384
CHANNELS = 256
WINDOWS = 8
NBLK = 32
PAIRS = 64
TILES = 16
OWNERS = 4


def draw_raw_samples(key, part):
    keys = jax.random.split(jax.random.fold_in(key, 3), 3)
    channel_scale = jnp.exp(jax.random.uniform(keys[1], (CHANNELS, 1, 1), jnp.float32, 0.0, math.log(10.0)))
    window_scale = jnp.exp(jax.random.uniform(keys[2], (1, WINDOWS, 1), jnp.float32, 0.0, math.log(3.0)))
    noise = jax.random.normal(keys[0], (CHANNELS, WINDOWS, RAW), jnp.float32)
    return (noise * channel_scale * window_scale).astype(jnp.bfloat16)


def draw_tile_pairs(key, part):
    first_key, second_key = jax.random.split(jax.random.fold_in(key, 7))
    source = jax.random.randint(first_key, (TILES,), 0, NBLK, dtype=jnp.int32)
    offset = jax.random.randint(second_key, (TILES,), 1, NBLK, dtype=jnp.int32)
    return jnp.stack([source, (source + offset) % NBLK], axis=1).astype(jnp.int32)


def draw_tile_owners(key, part):
    keys = jax.random.split(jax.random.fold_in(key, 11), 3)
    busiest = jax.random.randint(keys[0], (), 0, OWNERS, dtype=jnp.int32)
    offsets = jax.random.randint(keys[1], (SLOTS,), 1, OWNERS, dtype=jnp.int32)
    others = (busiest + offsets) % OWNERS
    listed = jnp.concatenate([jnp.full((SLOTS,), busiest, jnp.int32), others.astype(jnp.int32)])
    order = jax.random.permutation(keys[2], TILES)
    return listed[order].astype(jnp.int32)


def centred(own_key, dims, width, bound, kind=jnp.bfloat16):
    return jnp.clip(width * jax.random.normal(own_key, dims, jnp.float32), -bound, bound).astype(kind)


def setup_inputs(seed: int = 0) -> dict:
    arg_keys = jax.random.split(jax.random.key(seed), 5)
    return {
        "raw_samples": draw_raw_samples(jax.random.fold_in(arg_keys[4], 71), 0),
        "filter_taps": centred(arg_keys[1], (TAPS,), TAPS ** -0.5, 0.75, jnp.float32),
        "tile_pairs": draw_tile_pairs(jax.random.fold_in(arg_keys[4], 71), 0),
        "tile_owners": draw_tile_owners(jax.random.fold_in(arg_keys[4], 71), 0),
    }


water_level = 0.2
epsilon = 1e-06

def fir_tables(filter_taps, block_size):
    in_rows = jnp.arange(DECIM * block_size, dtype=jnp.int32)[:, None]
    out_cols = jnp.arange(block_size, dtype=jnp.int32)[None, :]
    this_index = DECIM * out_cols + DECIM - 1 - in_rows
    last_index = this_index + DECIM * block_size
    tap_count = filter_taps.shape[0]

    def taps_at(tap_index):
        inside = (tap_index >= 0) & (tap_index < tap_count)
        values = jnp.take(filter_taps, jnp.clip(tap_index, 0, tap_count - 1))
        return jnp.where(inside, values, jnp.zeros_like(values)).astype(jnp.bfloat16)
    return (taps_at(this_index), taps_at(last_index))

def decimate(samples, filter_taps):
    row_count, row_length = samples.shape
    block_size = min(128, row_length // DECIM)
    this_table, last_table = fir_tables(filter_taps, block_size)
    segments = samples.reshape(-1, DECIM * block_size)
    current = jnp.dot(segments, this_table, preferred_element_type=jnp.float32).reshape(row_count, -1, block_size)
    spilled = jnp.dot(segments, last_table, preferred_element_type=jnp.float32).reshape(row_count, -1, block_size)
    spilled = jnp.pad(spilled[:, :-1], ((0, 0), (1, 0), (0, 0)))
    return (current + spilled).reshape(row_count, -1).astype(jnp.bfloat16)

def dft_table(point_count, bin_count):
    sample_index = jnp.arange(point_count, dtype=jnp.int32)[:, None]
    frequency = 1 + jnp.arange(bin_count, dtype=jnp.int32)[None, :]
    angle = (sample_index * frequency % point_count).astype(jnp.float32) * (2.0 * math.pi / point_count)
    return jnp.concatenate([jnp.cos(angle), -jnp.sin(angle)], axis=1).astype(jnp.bfloat16)

def lag_table(point_count, bin_count, lag_count, window_count):
    frequency = 1 + jnp.arange(bin_count, dtype=jnp.int32)[:, None]
    shifted = jnp.arange(lag_count, dtype=jnp.int32)[None, :] - lag_count // 2 + point_count
    angle = (frequency * shifted % point_count).astype(jnp.float32) * (2.0 * math.pi / point_count)
    weight = 1.0 / math.sqrt(window_count * bin_count)
    return jnp.concatenate([jnp.cos(angle) * weight, -jnp.sin(angle) * weight], axis=0)

def smoother(bin_count, span_width):
    bin_index = jnp.arange(bin_count, dtype=jnp.int32)
    nearby = (jnp.abs(bin_index[:, None] - bin_index[None, :]) <= (span_width - 1) // 2).astype(jnp.float32)
    return nearby / lax.optimization_barrier(jnp.sum(nearby, axis=0, keepdims=True))

def whiten(decimated):
    spectrum = jnp.dot(decimated, dft_table(decimated.shape[1], NBINS), preferred_element_type=jnp.float32)
    real_part = spectrum[:, :NBINS]
    imag_part = spectrum[:, NBINS:]
    magnitude = jnp.sqrt(real_part * real_part + imag_part * imag_part)
    smooth = jnp.dot(magnitude, smoother(NBINS, SMOOTH), precision=lax.Precision.HIGHEST)
    floor_level = water_level * lax.optimization_barrier(jnp.mean(smooth, axis=1, keepdims=True)) + epsilon
    factor = 1.0 / (smooth + floor_level)
    return (spectrum * jnp.concatenate([factor, factor], axis=1)).astype(jnp.bfloat16)

def cross_spectra(source, target):
    highest = lax.Precision.HIGHEST
    src_real = source[..., :NBINS]
    src_imag = source[..., NBINS:]
    dst_real = target[..., :NBINS]
    dst_imag = target[..., NBINS:]
    real_sum = jnp.einsum('wif,wjf->ijf', src_real, dst_real, precision=highest) + jnp.einsum('wif,wjf->ijf', src_imag, dst_imag, precision=highest)
    imag_sum = jnp.einsum('wif,wjf->ijf', src_real, dst_imag, precision=highest) - jnp.einsum('wif,wjf->ijf', src_imag, dst_real, precision=highest)
    pair_count = source.shape[1] * target.shape[1]
    return jnp.concatenate([real_sum.reshape(pair_count, NBINS), imag_sum.reshape(pair_count, NBINS)], axis=1)

def reference(raw_samples, filter_taps, tile_pairs, tile_owners):

    def one_window(window_index):
        samples = lax.dynamic_index_in_dim(raw_samples, window_index, 1, keepdims=False)
        return whiten(decimate(samples, filter_taps))
    spectra = lax.map(one_window, jnp.arange(WINDOWS, dtype=jnp.int32))
    lag_basis = lag_table(NFFT, NBINS, LAGS, WINDOWS)

    def one_tile(tile_row):
        source = lax.dynamic_slice_in_dim(spectra, (tile_row[0] * BLK).astype(jnp.int32), BLK, 1).astype(jnp.float32)
        target = lax.dynamic_slice_in_dim(spectra, (tile_row[1] * BLK).astype(jnp.int32), BLK, 1).astype(jnp.float32)
        return jnp.dot(cross_spectra(source, target), lag_basis, precision=lax.Precision.HIGHEST)
    correlation = lax.map(one_tile, tile_pairs)
    owner_ids = jnp.arange(OWNERS, dtype=jnp.int32)
    owned_by = tile_owners[None, :] == owner_ids[:, None]
    rank_in_owner = jnp.cumsum(owned_by.astype(jnp.int32), axis=1) - 1
    slot_ids = jnp.arange(SLOTS, dtype=jnp.int32)
    select = (owned_by[:, None, :] & (rank_in_owner[:, None, :] == slot_ids[None, :, None])).astype(jnp.float32)
    stacks = jnp.einsum('ost,tpl->ospl', select, correlation, precision=lax.Precision.HIGHEST)
    return stacks.reshape(OWNERS * SLOTS, PAIRS, LAGS)
```

```python
import math

import jax
import jax.numpy as jnp
import ml_dtypes
import numpy as np
from jax import lax
from jax.sharding import PartitionSpec as P

NFFT = 4096
DECIM = 4
TAPS = 64
NBINS = 1024
HALF = 31
LAGS = 512
BLK = 8
SLOTS = 8
QUARTER = NFFT // 4
SEG = 128
WATER = 0.2
EPS = 1e-06
BF16 = ml_dtypes.bfloat16


def bins_in_order():
    return np.concatenate([np.arange(2, NBINS + 1, 2), np.arange(1, NBINS + 1, 2)])


def dft_tables():
    k = bins_in_order()
    angle = 2.0 * np.pi / NFFT * ((np.arange(QUARTER) + 0.5)[:, None] * k[None, :] % NFFT)
    return np.cos(angle).astype(BF16), (-np.sin(angle)).astype(BF16)


def smoother_tables():
    k = bins_in_order()
    near = np.abs(k[:, None] - k[None, :]) <= HALF
    return near.astype(BF16), (1.0 / near.sum(axis=0)).astype(np.float32)[None, :]


def lag_tables():
    k = bins_in_order()
    lag = np.arange(LAGS) - LAGS // 2
    angle = 2.0 * np.pi / NFFT * (k[:, None] * lag[None, :] % NFFT)
    return np.concatenate([np.cos(angle), -np.sin(angle)], axis=0).astype(BF16)


def fir_table(filter_taps):
    row = jnp.arange(DECIM * SEG + TAPS, dtype=jnp.int32)[:, None]
    col = jnp.arange(SEG, dtype=jnp.int32)[None, :]
    lead = col - row // DECIM + TAPS // DECIM
    by_phase = filter_taps.reshape(TAPS // DECIM, DECIM)[:, ::-1]
    columns = jnp.tile(by_phase.T, (row.shape[0] // DECIM, 1))
    table = jnp.zeros((row.shape[0], SEG), jnp.float32)
    for d in range(TAPS // DECIM):
        table = table + jnp.where(lead == d, columns[:, d : d + 1], 0.0)
    return table.astype(jnp.bfloat16)


def slot_lists(tile_pairs, tile_owners, owners):
    owner_ids = jnp.arange(owners, dtype=jnp.int32)
    slot_ids = jnp.arange(SLOTS, dtype=jnp.int32)
    owned = tile_owners[None, :] == owner_ids[:, None]
    order = jnp.arange(tile_owners.shape[0], dtype=jnp.int32)
    earlier = owned[:, None, :] & (order[None, :, None] > order[None, None, :])
    rank = jnp.sum(earlier.astype(jnp.int32), axis=2)
    pick = (owned[:, None, :] & (rank[:, None, :] == slot_ids[None, :, None])).astype(jnp.int32)
    chosen = jnp.sum(pick[:, :, :, None] * tile_pairs[None, None], axis=2)
    live = jnp.sum(pick, axis=2)
    return chosen.reshape(-1, 2), live.reshape(-1)


def plain_device(raw_samples, filter_taps, tile_pairs, tile_owners):
    wide = lax.axis_size("wide")
    narrow = lax.axis_size("narrow")
    devices = wide * narrow
    mine = NBINS // devices
    chan, windows, length = raw_samples.shape
    rows = chan * windows
    table = fir_table(filter_taps)
    segments = raw_samples.reshape(rows, -1, DECIM * SEG)
    before = jnp.pad(segments[:, :-1, -TAPS:], ((0, 0), (1, 0), (0, 0)))
    quarters = []
    for q in range(4):
        span = slice(q * QUARTER // SEG, (q + 1) * QUARTER // SEG)
        now = table if q % 2 == 0 else table[:, ::-1]
        part = jnp.dot(segments[:, span], now[TAPS:], preferred_element_type=jnp.float32) + jnp.dot(
            before[:, span], now[:TAPS], preferred_element_type=jnp.float32
        )
        if q % 2:
            part = part[:, ::-1]
        quarters.append(part.reshape(rows, QUARTER))
    q0, q1, q2, q3 = quarters
    even, even_back = q0 + q3, q1 + q2
    odd, odd_back = q0 - q3, q1 - q2
    cos_table, sin_table = dft_tables()
    half = NBINS // 2

    def dft(values, part):
        return jnp.dot(values.astype(jnp.bfloat16), part, preferred_element_type=jnp.float32)

    real = jnp.concatenate(
        [dft(even + even_back, cos_table[:, :half]), dft(even - even_back, cos_table[:, half:])], axis=1
    )
    imag = jnp.concatenate(
        [dft(odd - odd_back, sin_table[:, :half]), dft(odd + odd_back, sin_table[:, half:])], axis=1
    )
    near, share = smoother_tables()
    magnitude = jnp.sqrt(real * real + imag * imag)
    smooth = (
        jnp.dot(magnitude.astype(jnp.bfloat16), near, preferred_element_type=jnp.float32) * share
    )
    factor = 1.0 / (smooth + (WATER * jnp.mean(smooth, axis=1, keepdims=True) + EPS))
    white = jnp.stack([real * factor, imag * factor], axis=1).astype(jnp.bfloat16)
    white = white.reshape(chan, windows, 2, devices, mine)
    white = jnp.transpose(white, (3, 0, 1, 2, 4)).reshape(devices, rows, 2 * mine)
    blocks = lax.all_to_all(white, ("wide", "narrow"), split_axis=0, concat_axis=0, tiled=True)
    chosen, live = slot_lists(tile_pairs, tile_owners, narrow)
    block_ids = jnp.arange(devices, dtype=jnp.int32)

    def picked(block, count):
        one_hot = (block[:, None] == block_ids[None, :]) & (count[:, None] > 0)
        rows_of = jnp.dot(
            one_hot.astype(jnp.bfloat16),
            blocks.reshape(devices, -1),
            preferred_element_type=jnp.float32,
        )
        return rows_of.reshape(-1, chan, windows, 2, mine)

    source = picked(chosen[:, 0], live)
    target = picked(chosen[:, 1], live)
    sr, si = source[:, :, None, :, 0], source[:, :, None, :, 1]
    tr, ti = target[:, None, :, :, 0], target[:, None, :, :, 1]
    cross = jnp.stack(
        [jnp.sum(sr * tr + si * ti, axis=3), jnp.sum(sr * ti - si * tr, axis=3)], axis=3
    ).astype(jnp.bfloat16)
    pairs = BLK * BLK // wide
    cross = cross.reshape(narrow, SLOTS, wide, pairs, 2, mine)
    cross = jnp.transpose(cross, (2, 0, 1, 3, 4, 5)).reshape(devices, SLOTS * pairs, 2 * mine)
    got = lax.all_to_all(cross, ("wide", "narrow"), split_axis=0, concat_axis=0, tiled=True)
    got = jnp.transpose(got.reshape(devices, SLOTS * pairs, 2, mine), (1, 2, 0, 3))
    flat = got.reshape(SLOTS * pairs, 2 * NBINS)
    weight = 1.0 / math.sqrt(windows * NBINS)
    stacked = jnp.dot(flat, lag_tables(), preferred_element_type=jnp.float32) * weight
    return stacked.reshape(SLOTS, pairs, LAGS)


def solution(mesh):
    return jax.shard_map(
        plain_device,
        mesh=mesh,
        in_specs=(P(("wide", "narrow"), None, None), P(), P(), P()),
        out_specs=P("narrow", "wide", None),
        check_vma=False,
    )
```

```python
import functools
import math

import jax
import jax.numpy as jnp
import ml_dtypes
import numpy as np
from jax import lax
from jax.experimental import pallas as pl
from jax.experimental.pallas import tpu as pltpu
from jax.sharding import PartitionSpec as P

NFFT = 4096
DECIM = 4
TAPS = 64
NBINS = 1024
HALF = 31
LAGS = 512
BLK = 8
SLOTS = 8
QUARTER = NFFT // 4
SEG = 128
WATER = 0.2
EPS = 1e-06
BF16 = ml_dtypes.bfloat16


def bins_in_order():
    return np.concatenate([np.arange(2, NBINS + 1, 2), np.arange(1, NBINS + 1, 2)])


def dft_tables():
    k = bins_in_order()
    angle = 2.0 * np.pi / NFFT * ((np.arange(QUARTER) + 0.5)[:, None] * k[None, :] % NFFT)
    return np.cos(angle).astype(BF16), (-np.sin(angle)).astype(BF16)


def smoother_tables():
    k = bins_in_order()
    near = np.abs(k[:, None] - k[None, :]) <= HALF
    return near.astype(BF16), (1.0 / near.sum(axis=0)).astype(np.float32)[None, :]


def lag_tables():
    k = bins_in_order()
    lag = np.arange(LAGS) - LAGS // 2
    angle = 2.0 * np.pi / NFFT * (k[:, None] * lag[None, :] % NFFT)
    return np.concatenate([np.cos(angle), -np.sin(angle)], axis=0).astype(BF16)


def fir_table(filter_taps):
    row = jnp.arange(DECIM * SEG + TAPS, dtype=jnp.int32)[:, None]
    col = jnp.arange(SEG, dtype=jnp.int32)[None, :]
    lead = col - row // DECIM + TAPS // DECIM
    by_phase = filter_taps.reshape(TAPS // DECIM, DECIM)[:, ::-1]
    columns = jnp.tile(by_phase.T, (row.shape[0] // DECIM, 1))
    table = jnp.zeros((row.shape[0], SEG), jnp.float32)
    for d in range(TAPS // DECIM):
        table = table + jnp.where(lead == d, columns[:, d : d + 1], 0.0)
    return table.astype(jnp.bfloat16)


def slot_lists(tile_pairs, tile_owners, owners):
    owner_ids = jnp.arange(owners, dtype=jnp.int32)
    slot_ids = jnp.arange(SLOTS, dtype=jnp.int32)
    owned = tile_owners[None, :] == owner_ids[:, None]
    order = jnp.arange(tile_owners.shape[0], dtype=jnp.int32)
    earlier = owned[:, None, :] & (order[None, :, None] > order[None, None, :])
    rank = jnp.sum(earlier.astype(jnp.int32), axis=2)
    pick = (owned[:, None, :] & (rank[:, None, :] == slot_ids[None, :, None])).astype(jnp.int32)
    chosen = jnp.sum(pick[:, :, :, None] * tile_pairs[None, None], axis=2)
    live = jnp.sum(pick, axis=2)
    return chosen.reshape(-1, 2), live.reshape(-1)


def plain_device(raw_samples, filter_taps, tile_pairs, tile_owners):
    wide = lax.axis_size("wide")
    narrow = lax.axis_size("narrow")
    devices = wide * narrow
    mine = NBINS // devices
    chan, windows, length = raw_samples.shape
    rows = chan * windows
    table = fir_table(filter_taps)
    segments = raw_samples.reshape(rows, -1, DECIM * SEG)
    before = jnp.pad(segments[:, :-1, -TAPS:], ((0, 0), (1, 0), (0, 0)))
    quarters = []
    for q in range(4):
        span = slice(q * QUARTER // SEG, (q + 1) * QUARTER // SEG)
        now = table if q % 2 == 0 else table[:, ::-1]
        part = jnp.dot(segments[:, span], now[TAPS:], preferred_element_type=jnp.float32) + jnp.dot(
            before[:, span], now[:TAPS], preferred_element_type=jnp.float32
        )
        if q % 2:
            part = part[:, ::-1]
        quarters.append(part.reshape(rows, QUARTER))
    q0, q1, q2, q3 = quarters
    even, even_back = q0 + q3, q1 + q2
    odd, odd_back = q0 - q3, q1 - q2
    cos_table, sin_table = dft_tables()
    half = NBINS // 2

    def dft(values, part):
        return jnp.dot(values.astype(jnp.bfloat16), part, preferred_element_type=jnp.float32)

    real = jnp.concatenate(
        [dft(even + even_back, cos_table[:, :half]), dft(even - even_back, cos_table[:, half:])], axis=1
    )
    imag = jnp.concatenate(
        [dft(odd - odd_back, sin_table[:, :half]), dft(odd + odd_back, sin_table[:, half:])], axis=1
    )
    near, share = smoother_tables()
    magnitude = jnp.sqrt(real * real + imag * imag)
    smooth = (
        jnp.dot(magnitude.astype(jnp.bfloat16), near, preferred_element_type=jnp.float32) * share
    )
    factor = 1.0 / (smooth + (WATER * jnp.mean(smooth, axis=1, keepdims=True) + EPS))
    white = jnp.stack([real * factor, imag * factor], axis=1).astype(jnp.bfloat16)
    white = white.reshape(chan, windows, 2, devices, mine)
    white = jnp.transpose(white, (3, 0, 1, 2, 4)).reshape(devices, rows, 2 * mine)
    blocks = lax.all_to_all(white, ("wide", "narrow"), split_axis=0, concat_axis=0, tiled=True)
    chosen, live = slot_lists(tile_pairs, tile_owners, narrow)
    block_ids = jnp.arange(devices, dtype=jnp.int32)

    def picked(block, count):
        one_hot = (block[:, None] == block_ids[None, :]) & (count[:, None] > 0)
        rows_of = jnp.dot(
            one_hot.astype(jnp.bfloat16),
            blocks.reshape(devices, -1),
            preferred_element_type=jnp.float32,
        )
        return rows_of.reshape(-1, chan, windows, 2, mine)

    source = picked(chosen[:, 0], live)
    target = picked(chosen[:, 1], live)
    sr, si = source[:, :, None, :, 0], source[:, :, None, :, 1]
    tr, ti = target[:, None, :, :, 0], target[:, None, :, :, 1]
    cross = jnp.stack(
        [jnp.sum(sr * tr + si * ti, axis=3), jnp.sum(sr * ti - si * tr, axis=3)], axis=3
    ).astype(jnp.bfloat16)
    pairs = BLK * BLK // wide
    cross = cross.reshape(narrow, SLOTS, wide, pairs, 2, mine)
    cross = jnp.transpose(cross, (2, 0, 1, 3, 4, 5)).reshape(devices, SLOTS * pairs, 2 * mine)
    got = lax.all_to_all(cross, ("wide", "narrow"), split_axis=0, concat_axis=0, tiled=True)
    got = jnp.transpose(got.reshape(devices, SLOTS * pairs, 2, mine), (1, 2, 0, 3))
    flat = got.reshape(SLOTS * pairs, 2 * NBINS)
    weight = 1.0 / math.sqrt(windows * NBINS)
    stacked = jnp.dot(flat, lag_tables(), preferred_element_type=jnp.float32) * weight
    return stacked.reshape(SLOTS, pairs, LAGS)


WINDOWS = 8
DEVICES = 32
LANES = 128
MINE = NBINS // DEVICES
ROWS = BLK * WINDOWS
HALF_ROWS = ROWS // 2
SPAN = 2 * SEG
REACH = DECIM * SPAN + LANES
MESH = pl.DeviceIdType.MESH


def row_order():
    table = np.zeros((ROWS, ROWS), BF16)
    for window in range(WINDOWS):
        for chan in range(BLK):
            table[window * BLK + chan, chan * WINDOWS + window] = 1
    return table


def lane_order():
    table = np.zeros((4 * LANES, 4 * LANES), BF16)
    for kind in range(4):
        for dest in range(4):
            for b in range(MINE):
                table[kind * LANES + dest * MINE + b, dest * LANES + kind * MINE + b] = 1
    return table


def paired_lags():
    real, imag = np.split(lag_tables(), 2)
    width = 2 * MINE
    both = np.stack([real.reshape(-1, width, LAGS), imag.reshape(-1, width, LAGS)], axis=1)
    return both.reshape(2 * NBINS, LAGS)


def make_fir(taps, fir):
    fir[...] = jnp.zeros_like(fir)
    sub = lax.broadcasted_iota(jnp.int32, (8, LANES), 0)
    lane = lax.broadcasted_iota(jnp.int32, (8, LANES), 1)
    for back in range(2):
        spot = LANES - 1 - lane if back else lane
        number = DECIM * spot - 1 - sub
        base = jnp.zeros((8, LANES), jnp.float32)
        for k in range(TAPS):
            base = jnp.where(number == k, taps[k], base)

        def row_block(u):
            shift = 2 * u - 17
            moved = pltpu.roll(base, (-shift if back else shift) % LANES, 1)
            at = spot - shift
            return jnp.where((at >= 0) & (at < 18), moved, 0.0)

        for u in range(0, (DECIM * SEG + TAPS) // 8, 2):
            rows = jnp.concatenate([row_block(u), row_block(u + 1)], axis=0).astype(jnp.bfloat16)
            for seg in range(2):
                top = TAPS + seg * DECIM * SEG + 8 * u
                left = LANES * (1 - seg if back else seg)
                fir[back, top : top + 16, left : left + LANES] = rows


def local_part(raw, fir, tables, wait, send):
    cos_table, sin_table, near, share, rows_to, lanes_to = tables
    quarters = []
    for q in range(4):
        parts = []
        for n in range(4):
            first = (q * 4 + (3 - n if q % 2 else n)) * DECIM * SPAN
            if first:
                parts.append(raw[:, first - LANES : first + DECIM * SPAN])
            else:
                parts.append(
                    jnp.concatenate(
                        [jnp.zeros((ROWS, LANES), jnp.bfloat16), raw[:, : DECIM * SPAN]], axis=1
                    )
                )
        out = jnp.dot(
            jnp.concatenate(parts, axis=0), fir[q % 2], preferred_element_type=jnp.float32
        )
        quarters.append(
            jnp.concatenate([out[n * ROWS : (n + 1) * ROWS] for n in range(4)], axis=1)
        )
    q0, q1, q2, q3 = quarters
    even, even_back = q0 + q3, q1 + q2
    odd, odd_back = q0 - q3, q1 - q2
    half = NBINS // 2

    def dft(values, part):
        return jnp.dot(values.astype(jnp.bfloat16), part, preferred_element_type=jnp.float32)

    wait("cos")
    real = jnp.concatenate(
        [dft(even + even_back, cos_table[:, :half]), dft(even - even_back, cos_table[:, half:])],
        axis=1,
    )
    wait("sin")
    imag = jnp.concatenate(
        [dft(odd - odd_back, sin_table[:, :half]), dft(odd + odd_back, sin_table[:, half:])], axis=1
    )
    magnitude = jnp.sqrt(real * real + imag * imag).astype(jnp.bfloat16)
    wait("near")
    smooth = jnp.dot(magnitude, near[...], preferred_element_type=jnp.float32) * share[...]
    factor = 1.0 / (smooth + (WATER * jnp.mean(smooth, axis=1, keepdims=True) + EPS))
    wait("lanes")
    real = dft(rows_to[...], (real * factor).astype(jnp.bfloat16)).astype(jnp.bfloat16)
    imag = dft(rows_to[...], (imag * factor).astype(jnp.bfloat16)).astype(jnp.bfloat16)
    chunks = []
    for c in range(NBINS // LANES):
        cols = slice(c * LANES, (c + 1) * LANES)
        chunks.append(
            jnp.concatenate(
                [
                    real[:HALF_ROWS, cols],
                    imag[:HALF_ROWS, cols],
                    real[HALF_ROWS:, cols],
                    imag[HALF_ROWS:, cols],
                ],
                axis=1,
            )
        )
    moved = jnp.dot(
        jnp.concatenate(chunks, axis=0), lanes_to[...], preferred_element_type=jnp.float32
    ).astype(jnp.bfloat16)
    for p in range(DEVICES):
        top, left = p // 4 * HALF_ROWS, p % 4 * LANES
        send[p] = moved[top : top + HALF_ROWS, left : left + LANES]


def cross_part(first, second, live, blocks, send):
    lane = lax.broadcasted_iota(jnp.int32, (BLK, LANES), 1)
    low = lane % (2 * MINE) < MINE
    left = lane < LANES // 2
    lane32 = lax.broadcasted_iota(jnp.int32, (HALF_ROWS, LANES), 1)
    low32 = lane32 % (2 * MINE) < MINE

    def four_slots(step, _):
        owner, quad = step // 2, step % 2
        folded = [[None] * BLK for _ in range(4)]
        for n in range(4):
            slot = owner * SLOTS + quad * 4 + n
            source = blocks[first[slot]].astype(jnp.float32)
            target = blocks[second[slot]].astype(jnp.float32) * live[slot]
            turned = jnp.where(
                low32, pltpu.roll(target, LANES - MINE, 1), -pltpu.roll(target, MINE, 1)
            )
            for i in range(BLK):
                real = imag = None
                for w in range(4):
                    one = source[w * BLK + i : w * BLK + i + 1]
                    r = one * target[w * BLK : (w + 1) * BLK]
                    m = one * turned[w * BLK : (w + 1) * BLK]
                    real = r if real is None else real + r
                    imag = m if imag is None else imag + m
                both = jnp.where(
                    left,
                    real + pltpu.roll(real, LANES // 2, 1),
                    imag + pltpu.roll(imag, LANES // 2, 1),
                )
                folded[n][i] = both + pltpu.roll(both, MINE if n % 2 else LANES - MINE, 1)
        for i in range(BLK):
            upper = jnp.where(low, folded[0][i], folded[1][i])
            lower = jnp.where(low, folded[2][i], folded[3][i])
            send[i * 4 + owner, pl.ds(pl.multiple_of(quad * 16, 16), 16), :] = jnp.concatenate(
                [upper, lower], axis=0
            ).astype(jnp.bfloat16)
        return 0

    lax.fori_loop(0, 8, four_slots, 0)


def lag_part(got, lags, out, weight):
    lane = lax.broadcasted_iota(jnp.int32, (HALF_ROWS, LANES), 1)
    low = lane % (2 * MINE) < MINE
    even, odd = [], []
    for m in range(DEVICES // 2):
        one = got[2 * m].astype(jnp.float32)
        two = got[2 * m + 1].astype(jnp.float32)
        even.append(jnp.where(low, one, pltpu.roll(two, MINE, 1)))
        odd.append(jnp.where(low, pltpu.roll(one, LANES - MINE, 1), two))
    both = jnp.concatenate(
        [jnp.concatenate(even, axis=1), jnp.concatenate(odd, axis=1)], axis=0
    ).astype(jnp.bfloat16)
    result = jnp.dot(both, lags[...], preferred_element_type=jnp.float32) * weight
    for slot in range(SLOTS):
        top = slot % 2 * HALF_ROWS + slot // 2 * BLK
        out[slot] = result[top : top + BLK]


def everything(
    weight, taps, first, second, live, share, raw, cos_h, sin_h, near_h, rows_h, lanes_h, lags_h, out,
    raw_v, cos_v, sin_v, near_v, rows_v, lanes_v, lags_v, fir, send1, recv1, send2, recv2, load_sems,
    ssem1, rsem1, ssem2, rsem2,
):
    wide, narrow = lax.axis_index("wide"), lax.axis_index("narrow")
    me = wide * 4 + narrow
    barrier = pltpu.get_barrier_semaphore()

    def peer(d):
        p = lax.rem(me + d, DEVICES)
        return p, (p // 4, lax.rem(p, 4))

    def greet(d, _):
        pl.semaphore_signal(barrier, inc=1, device_id=peer(d)[1], device_id_type=MESH)
        return 0

    lax.fori_loop(1, DEVICES, greet, 0)
    pairs = [(raw, raw_v), (cos_h, cos_v), (sin_h, sin_v), (near_h, near_v), (rows_h, rows_v),
             (lanes_h, lanes_v), (lags_h, lags_v)]
    loads = [pltpu.make_async_copy(a, b, load_sems.at[n]) for n, (a, b) in enumerate(pairs)]
    for load in loads:
        load.start()
    make_fir(taps, fir)
    loads[0].wait()

    def wait(name):
        for n in {"cos": (1,), "sin": (2,), "near": (3,), "lanes": (4, 5)}[name]:
            loads[n].wait()

    local_part(raw_v, fir, (cos_v, sin_v, near_v, share, rows_v, lanes_v), wait, send1)
    pl.semaphore_wait(barrier, DEVICES - 1)

    def exchange(send, recv, ssem, rsem):
        def start(d, _):
            p, where = peer(d)
            pltpu.make_async_remote_copy(
                src_ref=send.at[p], dst_ref=recv.at[me], send_sem=ssem.at[p], recv_sem=rsem.at[me],
                device_id=where, device_id_type=MESH,
            ).start()
            return 0

        def finish(d, _):
            p, where = peer(d)
            pltpu.make_async_remote_copy(
                src_ref=send.at[p], dst_ref=recv.at[p], send_sem=ssem.at[p], recv_sem=rsem.at[p],
                device_id=where, device_id_type=MESH,
            ).wait()
            return 0

        lax.fori_loop(1, DEVICES, start, 0)
        recv[me] = send[me]
        lax.fori_loop(1, DEVICES, finish, 0)

    exchange(send1, recv1, ssem1, rsem1)
    cross_part(first, second, live, recv1, send2)
    exchange(send2, recv2, ssem2, rsem2)
    loads[6].wait()
    lag_part(recv2, lags_v, out, weight)


def fused_device(raw_samples, filter_taps, tile_pairs, tile_owners):
    raw = raw_samples.reshape(ROWS, -1)
    chosen, live = slot_lists(tile_pairs, tile_owners, 4)
    cos_table, sin_table = dft_tables()
    near, share = smoother_tables()
    held = [raw, cos_table, sin_table, near, row_order(), lane_order(), paired_lags()]
    smem = pl.BlockSpec(memory_space=pltpu.SMEM)
    vmem = pl.BlockSpec(memory_space=pltpu.VMEM)
    exchanged = pltpu.VMEM((DEVICES, HALF_ROWS, LANES), jnp.bfloat16)
    return pl.pallas_call(
        functools.partial(everything, 1.0 / math.sqrt(WINDOWS * NBINS)),
        out_shape=jax.ShapeDtypeStruct((SLOTS, BLK, LAGS), jnp.float32),
        in_specs=[smem] * 4 + [vmem] + [pl.BlockSpec(memory_space=pl.ANY)] * len(held),
        out_specs=vmem,
        scratch_shapes=[pltpu.VMEM(a.shape, jnp.bfloat16) for a in held]
        + [pltpu.VMEM((2, REACH, SPAN), jnp.bfloat16)]
        + [exchanged] * 4
        + [pltpu.SemaphoreType.DMA((len(held),))]
        + [pltpu.SemaphoreType.DMA((DEVICES,))] * 4,
        compiler_params=pltpu.CompilerParams(
            collective_id=0, has_side_effects=True, vmem_limit_bytes=50 * 2**20
        ),
    )(
        filter_taps, chosen[:, 0], chosen[:, 1], live.astype(jnp.float32), jnp.asarray(share),
        *(jnp.asarray(a) for a in held),
    )


def solution(mesh):
    fits = mesh.shape["wide"] == BLK and mesh.shape["narrow"] == 4

    def on_device(raw_samples, *rest):
        kept = fits and raw_samples.shape[:2] == (BLK, WINDOWS)
        return (fused_device if kept else plain_device)(raw_samples, *rest)

    return jax.shard_map(
        on_device,
        mesh=mesh,
        in_specs=(P(("wide", "narrow"), None, None), P(), P(), P()),
        out_specs=P("narrow", "wide", None),
        check_vma=False,
    )
```

```python
import functools
import math

import jax
import jax.numpy as jnp
import ml_dtypes
import numpy as np
from jax import lax
from jax.experimental import pallas as pl
from jax.experimental.pallas import tpu as pltpu
from jax.sharding import PartitionSpec as P

NFFT = 4096
DECIM = 4
TAPS = 64
NBINS = 1024
HALF = 31
LAGS = 512
BLK = 8
SLOTS = 8
QUARTER = NFFT // 4
SEG = 128
WATER = 0.2
EPS = 1e-06
BF16 = ml_dtypes.bfloat16


def bins_in_order():
    return np.concatenate([np.arange(2, NBINS + 1, 2), np.arange(1, NBINS + 1, 2)])


def dft_tables():
    k = bins_in_order()
    angle = 2.0 * np.pi / NFFT * ((np.arange(QUARTER) + 0.5)[:, None] * k[None, :] % NFFT)
    return np.cos(angle).astype(BF16), (-np.sin(angle)).astype(BF16)


def smoother_tables():
    k = bins_in_order()
    near = np.abs(k[:, None] - k[None, :]) <= HALF
    return near.astype(BF16), (1.0 / near.sum(axis=0)).astype(np.float32)[None, :]


def lag_tables():
    k = bins_in_order()
    lag = np.arange(LAGS) - LAGS // 2
    angle = 2.0 * np.pi / NFFT * (k[:, None] * lag[None, :] % NFFT)
    return np.concatenate([np.cos(angle), -np.sin(angle)], axis=0).astype(BF16)


def fir_table(filter_taps):
    row = jnp.arange(DECIM * SEG + TAPS, dtype=jnp.int32)[:, None]
    col = jnp.arange(SEG, dtype=jnp.int32)[None, :]
    lead = col - row // DECIM + TAPS // DECIM
    by_phase = filter_taps.reshape(TAPS // DECIM, DECIM)[:, ::-1]
    columns = jnp.tile(by_phase.T, (row.shape[0] // DECIM, 1))
    table = jnp.zeros((row.shape[0], SEG), jnp.float32)
    for d in range(TAPS // DECIM):
        table = table + jnp.where(lead == d, columns[:, d : d + 1], 0.0)
    return table.astype(jnp.bfloat16)


def slot_lists(tile_pairs, tile_owners, owners):
    owner_ids = jnp.arange(owners, dtype=jnp.int32)
    slot_ids = jnp.arange(SLOTS, dtype=jnp.int32)
    owned = tile_owners[None, :] == owner_ids[:, None]
    order = jnp.arange(tile_owners.shape[0], dtype=jnp.int32)
    earlier = owned[:, None, :] & (order[None, :, None] > order[None, None, :])
    rank = jnp.sum(earlier.astype(jnp.int32), axis=2)
    pick = (owned[:, None, :] & (rank[:, None, :] == slot_ids[None, :, None])).astype(jnp.int32)
    chosen = jnp.sum(pick[:, :, :, None] * tile_pairs[None, None], axis=2)
    live = jnp.sum(pick, axis=2)
    return chosen.reshape(-1, 2), live.reshape(-1)


def plain_device(raw_samples, filter_taps, tile_pairs, tile_owners):
    wide = lax.axis_size("wide")
    narrow = lax.axis_size("narrow")
    devices = wide * narrow
    mine = NBINS // devices
    chan, windows, length = raw_samples.shape
    rows = chan * windows
    table = fir_table(filter_taps)
    segments = raw_samples.reshape(rows, -1, DECIM * SEG)
    before = jnp.pad(segments[:, :-1, -TAPS:], ((0, 0), (1, 0), (0, 0)))
    quarters = []
    for q in range(4):
        span = slice(q * QUARTER // SEG, (q + 1) * QUARTER // SEG)
        now = table if q % 2 == 0 else table[:, ::-1]
        part = jnp.dot(segments[:, span], now[TAPS:], preferred_element_type=jnp.float32) + jnp.dot(
            before[:, span], now[:TAPS], preferred_element_type=jnp.float32
        )
        if q % 2:
            part = part[:, ::-1]
        quarters.append(part.reshape(rows, QUARTER))
    q0, q1, q2, q3 = quarters
    even, even_back = q0 + q3, q1 + q2
    odd, odd_back = q0 - q3, q1 - q2
    cos_table, sin_table = dft_tables()
    half = NBINS // 2

    def dft(values, part):
        return jnp.dot(values.astype(jnp.bfloat16), part, preferred_element_type=jnp.float32)

    real = jnp.concatenate(
        [dft(even + even_back, cos_table[:, :half]), dft(even - even_back, cos_table[:, half:])], axis=1
    )
    imag = jnp.concatenate(
        [dft(odd - odd_back, sin_table[:, :half]), dft(odd + odd_back, sin_table[:, half:])], axis=1
    )
    near, share = smoother_tables()
    magnitude = jnp.sqrt(real * real + imag * imag)
    smooth = (
        jnp.dot(magnitude.astype(jnp.bfloat16), near, preferred_element_type=jnp.float32) * share
    )
    factor = 1.0 / (smooth + (WATER * jnp.mean(smooth, axis=1, keepdims=True) + EPS))
    white = jnp.stack([real * factor, imag * factor], axis=1).astype(jnp.bfloat16)
    white = white.reshape(chan, windows, 2, devices, mine)
    white = jnp.transpose(white, (3, 0, 1, 2, 4)).reshape(devices, rows, 2 * mine)
    blocks = lax.all_to_all(white, ("wide", "narrow"), split_axis=0, concat_axis=0, tiled=True)
    chosen, live = slot_lists(tile_pairs, tile_owners, narrow)
    block_ids = jnp.arange(devices, dtype=jnp.int32)

    def picked(block, count):
        one_hot = (block[:, None] == block_ids[None, :]) & (count[:, None] > 0)
        rows_of = jnp.dot(
            one_hot.astype(jnp.bfloat16),
            blocks.reshape(devices, -1),
            preferred_element_type=jnp.float32,
        )
        return rows_of.reshape(-1, chan, windows, 2, mine)

    source = picked(chosen[:, 0], live)
    target = picked(chosen[:, 1], live)
    sr, si = source[:, :, None, :, 0], source[:, :, None, :, 1]
    tr, ti = target[:, None, :, :, 0], target[:, None, :, :, 1]
    cross = jnp.stack(
        [jnp.sum(sr * tr + si * ti, axis=3), jnp.sum(sr * ti - si * tr, axis=3)], axis=3
    ).astype(jnp.bfloat16)
    pairs = BLK * BLK // wide
    cross = cross.reshape(narrow, SLOTS, wide, pairs, 2, mine)
    cross = jnp.transpose(cross, (2, 0, 1, 3, 4, 5)).reshape(devices, SLOTS * pairs, 2 * mine)
    got = lax.all_to_all(cross, ("wide", "narrow"), split_axis=0, concat_axis=0, tiled=True)
    got = jnp.transpose(got.reshape(devices, SLOTS * pairs, 2, mine), (1, 2, 0, 3))
    flat = got.reshape(SLOTS * pairs, 2 * NBINS)
    weight = 1.0 / math.sqrt(windows * NBINS)
    stacked = jnp.dot(flat, lag_tables(), preferred_element_type=jnp.float32) * weight
    return stacked.reshape(SLOTS, pairs, LAGS)


WINDOWS = 8
DEVICES = 32
LANES = 128
MINE = NBINS // DEVICES
ROWS = BLK * WINDOWS
HALF_ROWS = ROWS // 2
SPAN = 2 * SEG
REACH = DECIM * SPAN + LANES
MESH = pl.DeviceIdType.MESH


def row_order():
    table = np.zeros((ROWS, ROWS), BF16)
    for window in range(WINDOWS):
        for chan in range(BLK):
            table[window * BLK + chan, chan * WINDOWS + window] = 1
    return table


def lane_order():
    table = np.zeros((4 * LANES, 4 * LANES), BF16)
    for kind in range(4):
        for dest in range(4):
            for b in range(MINE):
                table[kind * LANES + dest * MINE + b, dest * LANES + kind * MINE + b] = 1
    return table


def paired_lags():
    real, imag = np.split(lag_tables(), 2)
    width = 2 * MINE
    both = np.stack([real.reshape(-1, width, LAGS), imag.reshape(-1, width, LAGS)], axis=1)
    return both.reshape(2 * NBINS, LAGS)


def make_fir(taps, fir):
    fir[...] = jnp.zeros_like(fir)
    sub = lax.broadcasted_iota(jnp.int32, (8, LANES), 0)
    lane = lax.broadcasted_iota(jnp.int32, (8, LANES), 1)
    for back in range(2):
        spot = LANES - 1 - lane if back else lane
        number = DECIM * spot - 1 - sub
        base = jnp.zeros((8, LANES), jnp.float32)
        for k in range(TAPS):
            base = jnp.where(number == k, taps[k], base)

        def row_block(u):
            shift = 2 * u - 17
            moved = pltpu.roll(base, (-shift if back else shift) % LANES, 1)
            at = spot - shift
            return jnp.where((at >= 0) & (at < 18), moved, 0.0)

        for u in range(0, (DECIM * SEG + TAPS) // 8, 2):
            rows = jnp.concatenate([row_block(u), row_block(u + 1)], axis=0).astype(jnp.bfloat16)
            for seg in range(2):
                top = TAPS + seg * DECIM * SEG + 8 * u
                left = LANES * (1 - seg if back else seg)
                fir[back, top : top + 16, left : left + LANES] = rows


def local_part(raw, fir, tables, wait, send):
    cos_table, sin_table, near, share, rows_to, lanes_to = tables
    quarters = []
    for q in range(4):
        parts = []
        for n in range(4):
            first = (q * 4 + (3 - n if q % 2 else n)) * DECIM * SPAN
            if first:
                parts.append(raw[:, first - LANES : first + DECIM * SPAN])
            else:
                parts.append(
                    jnp.concatenate(
                        [jnp.zeros((ROWS, LANES), jnp.bfloat16), raw[:, : DECIM * SPAN]], axis=1
                    )
                )
        out = jnp.dot(
            jnp.concatenate(parts, axis=0), fir[q % 2], preferred_element_type=jnp.float32
        )
        quarters.append(
            jnp.concatenate([out[n * ROWS : (n + 1) * ROWS] for n in range(4)], axis=1)
        )
    q0, q1, q2, q3 = quarters
    even, even_back = q0 + q3, q1 + q2
    odd, odd_back = q0 - q3, q1 - q2
    half = NBINS // 2

    def dft(values, part):
        return jnp.dot(values.astype(jnp.bfloat16), part, preferred_element_type=jnp.float32)

    wait("cos")
    real = jnp.concatenate(
        [dft(even + even_back, cos_table[:, :half]), dft(even - even_back, cos_table[:, half:])],
        axis=1,
    )
    wait("sin")
    imag = jnp.concatenate(
        [dft(odd - odd_back, sin_table[:, :half]), dft(odd + odd_back, sin_table[:, half:])], axis=1
    )
    magnitude = jnp.sqrt(real * real + imag * imag).astype(jnp.bfloat16)
    wait("near")
    smooth = jnp.dot(magnitude, near[...], preferred_element_type=jnp.float32) * share[...]
    factor = 1.0 / (smooth + (WATER * jnp.mean(smooth, axis=1, keepdims=True) + EPS))
    wait("lanes")
    real = dft(rows_to[...], (real * factor).astype(jnp.bfloat16)).astype(jnp.bfloat16)
    imag = dft(rows_to[...], (imag * factor).astype(jnp.bfloat16)).astype(jnp.bfloat16)
    chunks = []
    for c in range(NBINS // LANES):
        cols = slice(c * LANES, (c + 1) * LANES)
        chunks.append(
            jnp.concatenate(
                [
                    real[:HALF_ROWS, cols],
                    imag[:HALF_ROWS, cols],
                    real[HALF_ROWS:, cols],
                    imag[HALF_ROWS:, cols],
                ],
                axis=1,
            )
        )
    moved = jnp.dot(
        jnp.concatenate(chunks, axis=0), lanes_to[...], preferred_element_type=jnp.float32
    ).astype(jnp.bfloat16)
    for p in range(DEVICES):
        top, left = p // 4 * HALF_ROWS, p % 4 * LANES
        send[p] = moved[top : top + HALF_ROWS, left : left + LANES]


def list_slots(pairs, owners, first, second, live):
    def one_slot(slot, _):
        owner, rank = slot // SLOTS, slot % SLOTS
        count = a = b = held = jnp.int32(0)
        for t in range(owners.shape[0]):
            mine = owners[t] == owner
            hit = mine & (count == rank)
            a = jnp.where(hit, pairs[t, 0], a)
            b = jnp.where(hit, pairs[t, 1], b)
            held = jnp.where(hit, 1, held)
            count = jnp.where(mine, count + 1, count)
        first[slot] = a
        second[slot] = b
        live[slot] = held.astype(jnp.float32)
        return 0

    lax.fori_loop(0, 4 * SLOTS, one_slot, 0)


def cross_part(first, second, live, blocks, send, owner_at, sent):
    lane = lax.broadcasted_iota(jnp.int32, (BLK, LANES), 1)
    low = lane % (2 * MINE) < MINE
    left = lane < LANES // 2
    lane32 = lax.broadcasted_iota(jnp.int32, (HALF_ROWS, LANES), 1)
    low32 = lane32 % (2 * MINE) < MINE

    def four_slots(owner, quad):
        folded = [[None] * BLK for _ in range(4)]
        for n in range(4):
            slot = owner * SLOTS + quad * 4 + n
            source = blocks[first[slot]].astype(jnp.float32)
            target = blocks[second[slot]].astype(jnp.float32) * live[slot]
            turned = jnp.where(
                low32, pltpu.roll(target, LANES - MINE, 1), -pltpu.roll(target, MINE, 1)
            )
            for i in range(BLK):
                real = imag = None
                for w in range(4):
                    one = source[w * BLK + i : w * BLK + i + 1]
                    r = one * target[w * BLK : (w + 1) * BLK]
                    m = one * turned[w * BLK : (w + 1) * BLK]
                    real = r if real is None else real + r
                    imag = m if imag is None else imag + m
                both = jnp.where(
                    left,
                    real + pltpu.roll(real, LANES // 2, 1),
                    imag + pltpu.roll(imag, LANES // 2, 1),
                )
                folded[n][i] = both + pltpu.roll(both, MINE if n % 2 else LANES - MINE, 1)
        for i in range(BLK):
            upper = jnp.where(low, folded[0][i], folded[1][i])
            lower = jnp.where(low, folded[2][i], folded[3][i])
            send[i * 4 + owner, pl.ds(pl.multiple_of(quad * 16, 16), 16), :] = jnp.concatenate(
                [upper, lower], axis=0
            ).astype(jnp.bfloat16)

    def one_owner(k, _):
        owner = owner_at(k)

        def half(quad, _):
            four_slots(owner, quad)
            return 0

        lax.fori_loop(0, 2, half, 0)
        sent(k)
        return 0

    lax.fori_loop(0, 4, one_owner, 0)


def lag_part(got, lags, out, weight):
    lane = lax.broadcasted_iota(jnp.int32, (HALF_ROWS, LANES), 1)
    low = lane % (2 * MINE) < MINE
    even, odd = [], []
    for m in range(DEVICES // 2):
        one = got[2 * m].astype(jnp.float32)
        two = got[2 * m + 1].astype(jnp.float32)
        even.append(jnp.where(low, one, pltpu.roll(two, MINE, 1)))
        odd.append(jnp.where(low, pltpu.roll(one, LANES - MINE, 1), two))
    both = jnp.concatenate(
        [jnp.concatenate(even, axis=1), jnp.concatenate(odd, axis=1)], axis=0
    ).astype(jnp.bfloat16)
    result = jnp.dot(both, lags[...], preferred_element_type=jnp.float32) * weight
    for slot in range(SLOTS):
        top = slot % 2 * HALF_ROWS + slot // 2 * BLK
        out[slot] = result[top : top + BLK]


def everything(
    weight, taps, pairs_s, owners_s, share, raw, cos_h, sin_h, near_h, rows_h, lanes_h, lags_h, out,
    raw_v, cos_v, sin_v, near_v, rows_v, lanes_v, lags_v, fir, send1, recv1, send2, recv2, load_sems,
    ssem1, rsem1, ssem2, rsem2, first, second, live,
):
    wide, narrow = lax.axis_index("wide"), lax.axis_index("narrow")
    me = wide * 4 + narrow
    barrier = pltpu.get_barrier_semaphore()

    def owner_at(k):
        return lax.rem(narrow + 1 + k, 4)

    def peer(d):
        to = (lax.rem(wide + lax.rem(d + 1, 8), 8), owner_at(d // 8))
        return to[0] * 4 + to[1], to

    def greet(d, _):
        pl.semaphore_signal(barrier, inc=1, device_id=peer(d)[1], device_id_type=MESH)
        return 0

    lax.fori_loop(0, DEVICES - 1, greet, 0)
    pairs = [(raw, raw_v), (cos_h, cos_v), (sin_h, sin_v), (near_h, near_v), (rows_h, rows_v),
             (lanes_h, lanes_v), (lags_h, lags_v)]
    loads = [pltpu.make_async_copy(a, b, load_sems.at[n]) for n, (a, b) in enumerate(pairs)]
    for load in loads:
        load.start()
    make_fir(taps, fir)
    loads[0].wait()

    def wait(name):
        for n in {"cos": (1,), "sin": (2,), "near": (3,), "lanes": (4, 5)}[name]:
            loads[n].wait()

    local_part(raw_v, fir, (cos_v, sin_v, near_v, share, rows_v, lanes_v), wait, send1)
    pl.semaphore_wait(barrier, DEVICES - 1)

    def copy(d, send, recv, ssem, rsem, at):
        p, where = peer(d)
        at = p if at is None else at
        return pltpu.make_async_remote_copy(
            src_ref=send.at[p], dst_ref=recv.at[at], send_sem=ssem.at[p], recv_sem=rsem.at[at],
            device_id=where, device_id_type=MESH,
        )

    one, two = (send1, recv1, ssem1, rsem1), (send2, recv2, ssem2, rsem2)

    def start1(d, _):
        copy(d, *one, me).start()
        return 0

    def finish1(d, _):
        copy(d, *one, None).wait()
        return 0

    def finish2(d, _):
        copy(d, *two, None).wait()
        return 0

    def sent(k):
        def start2(d, _):
            copy(d, *two, me).start()
            return 0

        lax.fori_loop(k * 8, jnp.minimum(k * 8 + 8, DEVICES - 1), start2, 0)

    lax.fori_loop(0, DEVICES - 1, start1, 0)
    recv1[me] = send1[me]
    list_slots(pairs_s, owners_s, first, second, live)
    lax.fori_loop(0, DEVICES - 1, finish1, 0)
    cross_part(first, second, live, recv1, send2, owner_at, sent)
    recv2[me] = send2[me]
    lax.fori_loop(0, DEVICES - 1, finish2, 0)
    loads[6].wait()
    lag_part(recv2, lags_v, out, weight)


def fused_device(raw_samples, filter_taps, tile_pairs, tile_owners):
    raw = raw_samples.reshape(ROWS, -1)
    cos_table, sin_table = dft_tables()
    near, share = smoother_tables()
    held = [raw, cos_table, sin_table, near, row_order(), lane_order(), paired_lags()]
    smem = pl.BlockSpec(memory_space=pltpu.SMEM)
    vmem = pl.BlockSpec(memory_space=pltpu.VMEM)
    exchanged = pltpu.VMEM((DEVICES, HALF_ROWS, LANES), jnp.bfloat16)
    return pl.pallas_call(
        functools.partial(everything, 1.0 / math.sqrt(WINDOWS * NBINS)),
        out_shape=jax.ShapeDtypeStruct((SLOTS, BLK, LAGS), jnp.float32),
        in_specs=[smem] * 3 + [vmem] + [pl.BlockSpec(memory_space=pl.ANY)] * len(held),
        out_specs=vmem,
        scratch_shapes=[pltpu.VMEM(a.shape, jnp.bfloat16) for a in held]
        + [pltpu.VMEM((2, REACH, SPAN), jnp.bfloat16)]
        + [exchanged] * 4
        + [pltpu.SemaphoreType.DMA((len(held),))]
        + [pltpu.SemaphoreType.DMA((DEVICES,))] * 4
        + [pltpu.SMEM((4 * SLOTS,), kind) for kind in (jnp.int32, jnp.int32, jnp.float32)],
        compiler_params=pltpu.CompilerParams(
            collective_id=0, has_side_effects=True, vmem_limit_bytes=60 * 2**20
        ),
    )(
        filter_taps, tile_pairs, tile_owners, jnp.asarray(share),
        *(jnp.asarray(a) for a in held),
    )


def solution(mesh):
    fits = mesh.shape["wide"] == BLK and mesh.shape["narrow"] == 4

    def on_device(raw_samples, *rest):
        kept = fits and raw_samples.shape[:2] == (BLK, WINDOWS)
        return (fused_device if kept else plain_device)(raw_samples, *rest)

    return jax.shard_map(
        on_device,
        mesh=mesh,
        in_specs=(P(("wide", "narrow"), None, None), P(), P(), P()),
        out_specs=P("narrow", "wide", None),
        check_vma=False,
    )
```

```python
import functools
import math

import jax
import jax.numpy as jnp
import ml_dtypes
import numpy as np
from jax import lax
from jax.experimental import pallas as pl
from jax.experimental.pallas import tpu as pltpu
from jax.sharding import PartitionSpec as P

NFFT = 4096
DECIM = 4
TAPS = 64
NBINS = 1024
HALF = 31
LAGS = 512
BLK = 8
SLOTS = 8
QUARTER = NFFT // 4
SEG = 128
WATER = 0.2
EPS = 1e-06
BF16 = ml_dtypes.bfloat16


def bins_in_order():
    return np.concatenate([np.arange(2, NBINS + 1, 2), np.arange(1, NBINS + 1, 2)])


def dft_tables():
    k = bins_in_order()
    angle = 2.0 * np.pi / NFFT * ((np.arange(QUARTER) + 0.5)[:, None] * k[None, :] % NFFT)
    return np.cos(angle).astype(BF16), (-np.sin(angle)).astype(BF16)


def smoother_tables():
    k = bins_in_order()
    near = np.abs(k[:, None] - k[None, :]) <= HALF
    return near.astype(BF16), (1.0 / near.sum(axis=0)).astype(np.float32)[None, :]


def lag_tables():
    k = bins_in_order()
    lag = np.arange(LAGS) - LAGS // 2
    angle = 2.0 * np.pi / NFFT * (k[:, None] * lag[None, :] % NFFT)
    return np.concatenate([np.cos(angle), -np.sin(angle)], axis=0).astype(BF16)


def fir_table(filter_taps):
    row = jnp.arange(DECIM * SEG + TAPS, dtype=jnp.int32)[:, None]
    col = jnp.arange(SEG, dtype=jnp.int32)[None, :]
    lead = col - row // DECIM + TAPS // DECIM
    by_phase = filter_taps.reshape(TAPS // DECIM, DECIM)[:, ::-1]
    columns = jnp.tile(by_phase.T, (row.shape[0] // DECIM, 1))
    table = jnp.zeros((row.shape[0], SEG), jnp.float32)
    for d in range(TAPS // DECIM):
        table = table + jnp.where(lead == d, columns[:, d : d + 1], 0.0)
    return table.astype(jnp.bfloat16)


def slot_lists(tile_pairs, tile_owners, owners):
    owner_ids = jnp.arange(owners, dtype=jnp.int32)
    slot_ids = jnp.arange(SLOTS, dtype=jnp.int32)
    owned = tile_owners[None, :] == owner_ids[:, None]
    order = jnp.arange(tile_owners.shape[0], dtype=jnp.int32)
    earlier = owned[:, None, :] & (order[None, :, None] > order[None, None, :])
    rank = jnp.sum(earlier.astype(jnp.int32), axis=2)
    pick = (owned[:, None, :] & (rank[:, None, :] == slot_ids[None, :, None])).astype(jnp.int32)
    chosen = jnp.sum(pick[:, :, :, None] * tile_pairs[None, None], axis=2)
    live = jnp.sum(pick, axis=2)
    return chosen.reshape(-1, 2), live.reshape(-1)


def plain_device(raw_samples, filter_taps, tile_pairs, tile_owners):
    wide = lax.axis_size("wide")
    narrow = lax.axis_size("narrow")
    devices = wide * narrow
    mine = NBINS // devices
    chan, windows, length = raw_samples.shape
    rows = chan * windows
    table = fir_table(filter_taps)
    segments = raw_samples.reshape(rows, -1, DECIM * SEG)
    before = jnp.pad(segments[:, :-1, -TAPS:], ((0, 0), (1, 0), (0, 0)))
    quarters = []
    for q in range(4):
        span = slice(q * QUARTER // SEG, (q + 1) * QUARTER // SEG)
        now = table if q % 2 == 0 else table[:, ::-1]
        part = jnp.dot(segments[:, span], now[TAPS:], preferred_element_type=jnp.float32) + jnp.dot(
            before[:, span], now[:TAPS], preferred_element_type=jnp.float32
        )
        if q % 2:
            part = part[:, ::-1]
        quarters.append(part.reshape(rows, QUARTER))
    q0, q1, q2, q3 = quarters
    even, even_back = q0 + q3, q1 + q2
    odd, odd_back = q0 - q3, q1 - q2
    cos_table, sin_table = dft_tables()
    half = NBINS // 2

    def dft(values, part):
        return jnp.dot(values.astype(jnp.bfloat16), part, preferred_element_type=jnp.float32)

    real = jnp.concatenate(
        [dft(even + even_back, cos_table[:, :half]), dft(even - even_back, cos_table[:, half:])], axis=1
    )
    imag = jnp.concatenate(
        [dft(odd - odd_back, sin_table[:, :half]), dft(odd + odd_back, sin_table[:, half:])], axis=1
    )
    near, share = smoother_tables()
    magnitude = jnp.sqrt(real * real + imag * imag)
    smooth = (
        jnp.dot(magnitude.astype(jnp.bfloat16), near, preferred_element_type=jnp.float32) * share
    )
    factor = 1.0 / (smooth + (WATER * jnp.mean(smooth, axis=1, keepdims=True) + EPS))
    white = jnp.stack([real * factor, imag * factor], axis=1).astype(jnp.bfloat16)
    white = white.reshape(chan, windows, 2, devices, mine)
    white = jnp.transpose(white, (3, 0, 1, 2, 4)).reshape(devices, rows, 2 * mine)
    blocks = lax.all_to_all(white, ("wide", "narrow"), split_axis=0, concat_axis=0, tiled=True)
    chosen, live = slot_lists(tile_pairs, tile_owners, narrow)
    block_ids = jnp.arange(devices, dtype=jnp.int32)

    def picked(block, count):
        one_hot = (block[:, None] == block_ids[None, :]) & (count[:, None] > 0)
        rows_of = jnp.dot(
            one_hot.astype(jnp.bfloat16),
            blocks.reshape(devices, -1),
            preferred_element_type=jnp.float32,
        )
        return rows_of.reshape(-1, chan, windows, 2, mine)

    source = picked(chosen[:, 0], live)
    target = picked(chosen[:, 1], live)
    sr, si = source[:, :, None, :, 0], source[:, :, None, :, 1]
    tr, ti = target[:, None, :, :, 0], target[:, None, :, :, 1]
    cross = jnp.stack(
        [jnp.sum(sr * tr + si * ti, axis=3), jnp.sum(sr * ti - si * tr, axis=3)], axis=3
    ).astype(jnp.bfloat16)
    pairs = BLK * BLK // wide
    cross = cross.reshape(narrow, SLOTS, wide, pairs, 2, mine)
    cross = jnp.transpose(cross, (2, 0, 1, 3, 4, 5)).reshape(devices, SLOTS * pairs, 2 * mine)
    got = lax.all_to_all(cross, ("wide", "narrow"), split_axis=0, concat_axis=0, tiled=True)
    got = jnp.transpose(got.reshape(devices, SLOTS * pairs, 2, mine), (1, 2, 0, 3))
    flat = got.reshape(SLOTS * pairs, 2 * NBINS)
    weight = 1.0 / math.sqrt(windows * NBINS)
    stacked = jnp.dot(flat, lag_tables(), preferred_element_type=jnp.float32) * weight
    return stacked.reshape(SLOTS, pairs, LAGS)


WINDOWS = 8
DEVICES = 32
LANES = 128
MINE = NBINS // DEVICES
ROWS = BLK * WINDOWS
HALF_ROWS = ROWS // 2
SPAN = 2 * SEG
REACH = DECIM * SPAN + LANES
MESH = pl.DeviceIdType.MESH


def row_order():
    table = np.zeros((ROWS, ROWS), BF16)
    for window in range(WINDOWS):
        for chan in range(BLK):
            table[window * BLK + chan, chan * WINDOWS + window] = 1
    return table


def lane_order():
    table = np.zeros((4 * LANES, 4 * LANES), BF16)
    for kind in range(4):
        for dest in range(4):
            for b in range(MINE):
                table[kind * LANES + dest * MINE + b, dest * LANES + kind * MINE + b] = 1
    return table


def paired_lags():
    real, imag = np.split(lag_tables(), 2)
    width = 2 * MINE
    both = np.stack([real.reshape(-1, width, LAGS), imag.reshape(-1, width, LAGS)], axis=1)
    return both.reshape(2 * NBINS, LAGS)


def make_fir(taps, fir):
    fir[...] = jnp.zeros_like(fir)
    sub = lax.broadcasted_iota(jnp.int32, (8, LANES), 0)
    lane = lax.broadcasted_iota(jnp.int32, (8, LANES), 1)
    for back in range(2):
        spot = LANES - 1 - lane if back else lane
        number = DECIM * spot - 1 - sub
        base = jnp.zeros((8, LANES), jnp.float32)
        for k in range(TAPS):
            base = jnp.where(number == k, taps[k], base)

        def row_block(u):
            shift = 2 * u - 17
            moved = pltpu.roll(base, (-shift if back else shift) % LANES, 1)
            at = spot - shift
            return jnp.where((at >= 0) & (at < 18), moved, 0.0)

        for u in range(0, (DECIM * SEG + TAPS) // 8, 2):
            rows = jnp.concatenate([row_block(u), row_block(u + 1)], axis=0).astype(jnp.bfloat16)
            for seg in range(2):
                top = TAPS + seg * DECIM * SEG + 8 * u
                left = LANES * (1 - seg if back else seg)
                fir[back, top : top + 16, left : left + LANES] = rows


def local_part(raw, fir, tables, wait, send):
    cos_table, sin_table, near, share, rows_to, lanes_to = tables
    quarters = []
    for q in range(4):
        parts = []
        for n in range(4):
            first = (q * 4 + (3 - n if q % 2 else n)) * DECIM * SPAN
            if first:
                parts.append(raw[:, first - LANES : first + DECIM * SPAN])
            else:
                parts.append(
                    jnp.concatenate(
                        [jnp.zeros((ROWS, LANES), jnp.bfloat16), raw[:, : DECIM * SPAN]], axis=1
                    )
                )
        out = jnp.dot(
            jnp.concatenate(parts, axis=0), fir[q % 2], preferred_element_type=jnp.float32
        )
        quarters.append(
            jnp.concatenate([out[n * ROWS : (n + 1) * ROWS] for n in range(4)], axis=1)
        )
    q0, q1, q2, q3 = quarters
    even, even_back = q0 + q3, q1 + q2
    odd, odd_back = q0 - q3, q1 - q2
    half = NBINS // 2

    def dft(values, part):
        return jnp.dot(values.astype(jnp.bfloat16), part, preferred_element_type=jnp.float32)

    wait("cos")
    real = jnp.concatenate(
        [dft(even + even_back, cos_table[:, :half]), dft(even - even_back, cos_table[:, half:])],
        axis=1,
    )
    wait("sin")
    imag = jnp.concatenate(
        [dft(odd - odd_back, sin_table[:, :half]), dft(odd + odd_back, sin_table[:, half:])], axis=1
    )
    magnitude = jnp.sqrt(real * real + imag * imag).astype(jnp.bfloat16)
    wait("near")
    smooth = jnp.dot(magnitude, near[...], preferred_element_type=jnp.float32) * share[...]
    factor = 1.0 / (smooth + (WATER * jnp.mean(smooth, axis=1, keepdims=True) + EPS))
    wait("lanes")
    real = dft(rows_to[...], (real * factor).astype(jnp.bfloat16)).astype(jnp.bfloat16)
    imag = dft(rows_to[...], (imag * factor).astype(jnp.bfloat16)).astype(jnp.bfloat16)
    chunks = []
    for c in range(NBINS // LANES):
        cols = slice(c * LANES, (c + 1) * LANES)
        chunks.append(
            jnp.concatenate(
                [
                    real[:HALF_ROWS, cols],
                    imag[:HALF_ROWS, cols],
                    real[HALF_ROWS:, cols],
                    imag[HALF_ROWS:, cols],
                ],
                axis=1,
            )
        )
    moved = jnp.dot(
        jnp.concatenate(chunks, axis=0), lanes_to[...], preferred_element_type=jnp.float32
    ).astype(jnp.bfloat16)
    for p in range(DEVICES):
        top, left = p // 4 * HALF_ROWS, p % 4 * LANES
        send[p] = moved[top : top + HALF_ROWS, left : left + LANES]


def list_slots(pairs, owners, first, second, live):
    def one_slot(slot, _):
        owner, rank = slot // SLOTS, slot % SLOTS
        count = a = b = held = jnp.int32(0)
        for t in range(owners.shape[0]):
            mine = owners[t] == owner
            hit = mine & (count == rank)
            a = jnp.where(hit, pairs[t, 0], a)
            b = jnp.where(hit, pairs[t, 1], b)
            held = jnp.where(hit, 1, held)
            count = jnp.where(mine, count + 1, count)
        first[slot] = a
        second[slot] = b
        live[slot] = held.astype(jnp.float32)
        return 0

    lax.fori_loop(0, 4 * SLOTS, one_slot, 0)


def cross_part(first, second, live, blocks, send, owner_at, sent):
    lane = lax.broadcasted_iota(jnp.int32, (BLK, LANES), 1)
    low = lane % (2 * MINE) < MINE
    left = lane < LANES // 2
    lane32 = lax.broadcasted_iota(jnp.int32, (HALF_ROWS, LANES), 1)
    low32 = lane32 % (2 * MINE) < MINE

    def four_slots(owner, quad):
        folded = [[None] * BLK for _ in range(4)]
        for n in range(4):
            slot = owner * SLOTS + quad * 4 + n
            source = blocks[first[slot]].astype(jnp.float32)
            target = blocks[second[slot]].astype(jnp.float32) * live[slot]
            turned = jnp.where(
                low32, pltpu.roll(target, LANES - MINE, 1), -pltpu.roll(target, MINE, 1)
            )
            for i in range(BLK):
                real = imag = None
                for w in range(4):
                    one = source[w * BLK + i : w * BLK + i + 1]
                    r = one * target[w * BLK : (w + 1) * BLK]
                    m = one * turned[w * BLK : (w + 1) * BLK]
                    real = r if real is None else real + r
                    imag = m if imag is None else imag + m
                both = jnp.where(
                    left,
                    real + pltpu.roll(real, LANES // 2, 1),
                    imag + pltpu.roll(imag, LANES // 2, 1),
                )
                folded[n][i] = both + pltpu.roll(both, MINE if n % 2 else LANES - MINE, 1)
        for i in range(BLK):
            upper = jnp.where(low, folded[0][i], folded[1][i])
            lower = jnp.where(low, folded[2][i], folded[3][i])
            send[i * 4 + owner, pl.ds(pl.multiple_of(quad * 16, 16), 16), :] = jnp.concatenate(
                [upper, lower], axis=0
            ).astype(jnp.bfloat16)

    def one_owner(k, _):
        owner = owner_at(k)

        def half(quad, _):
            four_slots(owner, quad)
            return 0

        lax.fori_loop(0, 2, half, 0)
        sent(k)
        return 0

    lax.fori_loop(0, 4, one_owner, 0)


def lag_part(got, lags, out, weight):
    lane = lax.broadcasted_iota(jnp.int32, (HALF_ROWS, LANES), 1)
    low = lane % (2 * MINE) < MINE
    even, odd = [], []
    for m in range(DEVICES // 2):
        one = got[2 * m].astype(jnp.float32)
        two = got[2 * m + 1].astype(jnp.float32)
        even.append(jnp.where(low, one, pltpu.roll(two, MINE, 1)))
        odd.append(jnp.where(low, pltpu.roll(one, LANES - MINE, 1), two))
    both = jnp.concatenate(
        [jnp.concatenate(even, axis=1), jnp.concatenate(odd, axis=1)], axis=0
    ).astype(jnp.bfloat16)
    result = jnp.dot(both, lags[...], preferred_element_type=jnp.float32) * weight
    for slot in range(SLOTS):
        top = slot % 2 * HALF_ROWS + slot // 2 * BLK
        out[slot] = result[top : top + BLK]


def everything(
    weight, taps, pairs_s, owners_s, share, raw, cos_h, sin_h, near_h, rows_h, lanes_h, lags_h, out,
    raw_v, cos_v, sin_v, near_v, rows_v, lanes_v, lags_v, fir, send1, recv1, send2, recv2, load_sems,
    ssem1, rsem1, ssem2, rsem2, first, second, live,
):
    wide, narrow = lax.axis_index("wide"), lax.axis_index("narrow")
    me = wide * 4 + narrow
    barrier = pltpu.get_barrier_semaphore()

    def owner_at(k):
        return lax.rem(narrow + 1 + k, 4)

    def peer(d):
        to = (lax.rem(wide + lax.rem(d + 1, 8), 8), owner_at(d // 8))
        return to[0] * 4 + to[1], to

    def greet(d, _):
        pl.semaphore_signal(barrier, inc=1, device_id=peer(d)[1], device_id_type=MESH)
        return 0

    pairs = [(raw, raw_v), (cos_h, cos_v), (sin_h, sin_v), (near_h, near_v), (rows_h, rows_v),
             (lanes_h, lanes_v), (lags_h, lags_v)]
    loads = [pltpu.make_async_copy(a, b, load_sems.at[n]) for n, (a, b) in enumerate(pairs)]
    for load in loads:
        load.start()
    lax.fori_loop(0, DEVICES - 1, greet, 0)
    make_fir(taps, fir)
    loads[0].wait()

    def wait(name):
        for n in {"cos": (1,), "sin": (2,), "near": (3,), "lanes": (4, 5)}[name]:
            loads[n].wait()

    local_part(raw_v, fir, (cos_v, sin_v, near_v, share, rows_v, lanes_v), wait, send1)
    pl.semaphore_wait(barrier, DEVICES - 1)

    def copy(d, send, recv, ssem, rsem, at):
        p, where = peer(d)
        at = p if at is None else at
        return pltpu.make_async_remote_copy(
            src_ref=send.at[p], dst_ref=recv.at[at], send_sem=ssem.at[p], recv_sem=rsem.at[at],
            device_id=where, device_id_type=MESH,
        )

    one, two = (send1, recv1, ssem1, rsem1), (send2, recv2, ssem2, rsem2)

    def start1(d, _):
        copy(d, *one, me).start()
        return 0

    def finish1(d, _):
        copy(d, *one, None).wait()
        return 0

    def finish2(d, _):
        copy(d, *two, None).wait()
        return 0

    def sent(k):
        def start2(d, _):
            copy(d, *two, me).start()
            return 0

        lax.fori_loop(k * 8, jnp.minimum(k * 8 + 8, DEVICES - 1), start2, 0)

    lax.fori_loop(0, DEVICES - 1, start1, 0)
    recv1[me] = send1[me]
    list_slots(pairs_s, owners_s, first, second, live)
    lax.fori_loop(0, DEVICES - 1, finish1, 0)
    cross_part(first, second, live, recv1, send2, owner_at, sent)
    recv2[me] = send2[me]
    lax.fori_loop(0, DEVICES - 1, finish2, 0)
    loads[6].wait()
    lag_part(recv2, lags_v, out, weight)


def fused_device(raw_samples, filter_taps, tile_pairs, tile_owners):
    raw = raw_samples.reshape(ROWS, -1)
    cos_table, sin_table = dft_tables()
    near, share = smoother_tables()
    held = [raw, cos_table, sin_table, near, row_order(), lane_order(), paired_lags()]
    smem = pl.BlockSpec(memory_space=pltpu.SMEM)
    vmem = pl.BlockSpec(memory_space=pltpu.VMEM)
    exchanged = pltpu.VMEM((DEVICES, HALF_ROWS, LANES), jnp.bfloat16)
    return pl.pallas_call(
        functools.partial(everything, 1.0 / math.sqrt(WINDOWS * NBINS)),
        out_shape=jax.ShapeDtypeStruct((SLOTS, BLK, LAGS), jnp.float32),
        in_specs=[smem] * 3 + [vmem] + [pl.BlockSpec(memory_space=pl.ANY)] * len(held),
        out_specs=vmem,
        scratch_shapes=[pltpu.VMEM(a.shape, jnp.bfloat16) for a in held]
        + [pltpu.VMEM((2, REACH, SPAN), jnp.bfloat16)]
        + [exchanged] * 4
        + [pltpu.SemaphoreType.DMA((len(held),))]
        + [pltpu.SemaphoreType.DMA((DEVICES,))] * 4
        + [pltpu.SMEM((4 * SLOTS,), kind) for kind in (jnp.int32, jnp.int32, jnp.float32)],
        compiler_params=pltpu.CompilerParams(
            collective_id=0, has_side_effects=True, vmem_limit_bytes=60 * 2**20
        ),
    )(
        filter_taps, tile_pairs, tile_owners, jnp.asarray(share),
        *(jnp.asarray(a) for a in held),
    )


def solution(mesh):
    fits = mesh.shape["wide"] == BLK and mesh.shape["narrow"] == 4

    def on_device(raw_samples, *rest):
        kept = fits and raw_samples.shape[:2] == (BLK, WINDOWS)
        return (fused_device if kept else plain_device)(raw_samples, *rest)

    return jax.shard_map(
        on_device,
        mesh=mesh,
        in_specs=(P(("wide", "narrow"), None, None), P(), P(), P()),
        out_specs=P("narrow", "wide", None),
        check_vma=False,
    )
```
